32 devices in a mesh: days: 2 (over x), blk: 16 (over z, y, core).
Axes of the slice: x: 2, y: 2, z: 4, core: 2. Of those that a mesh axis runs over, the one named last changes fastest.
Arguments:
- traces: bfloat16 [2048, 8, 1024], P(('days', 'blk')), parts along dimension 0, may hold values from -6 to 6
- valid: int32 [32, 8], P(('days', 'blk')), parts along dimension 0, may hold values from 0 to 1, as said below
Outputs:
- correlations: bfloat16 [2, 32, 64, 64, 512], P(None, ('days', 'blk')), parts along dimension 1
The draws below stay inside these ranges and needn't reach their ends.
There are 2 independent parts, one for each index of `days`. The reference program is written for one: setup_inputs(seed, part) draws one part's arguments, and reference() takes and returns one part's arrays. A program takes and returns all parts, laid end to end along the dimension named above; each array names one. Nothing has to cross between parts.
Inputs may be any that keep to these rules, and one draw needn't show every extreme that they name: `valid`: in every draw one block, which one is drawn from the seed, has no usable window at all.
All inputs are finite; a program needn't handle non-finite values.
Results may differ from the reference program's by a relative error of at most 0.0089.
Values may be sent and summed in bfloat16 or wider, within the bound.
No kernel may reach another device: no remote copies, remote signals or barrier semaphores. Data moves between devices by JAX's collectives and lax.ppermute only.
A program may use at most 128 MiB of HBM per device.

```python
import math
import jax
import jax.numpy as jnp
from jax import lax

CH = 64
WINDOW_SAMPLES = 1024
LAGS = 512
BAND = 64
ROUNDS = 2
TIME_WINDOWS = 8
FREQS = 512
BLOCKS = 16
CHANNELS = 1024


def draw_valid(key, part):
    mask_key = jax.random.fold_in(key, 11)
    pick_key = jax.random.fold_in(key, 23)
    levels = jax.random.randint(mask_key, (BLOCKS, TIME_WINDOWS), 0, 4, dtype=jnp.int32)
    usable = jnp.where(levels < 3, 1, 0).astype(jnp.int32)
    silent = jax.random.randint(pick_key, (), 0, BLOCKS, dtype=jnp.int32)
    rows = jnp.arange(BLOCKS, dtype=jnp.int32)[:, None]
    return jnp.where(rows == silent, 0, usable).astype(jnp.int32)


def shard_levels(key, extent, pieces, low, largest):
    level, own = 1.0, jax.random.fold_in(key, 6)
    for position, parts in pieces:
        draws = jnp.exp(jax.random.uniform(jax.random.fold_in(own, position), (parts,), jnp.float32, low / len(pieces), largest / len(pieces)))
        level = level * jnp.repeat(draws, extent[position] // parts).reshape([-1 if axis == position else 1 for axis in range(len(extent))])
    return level


def noise(own_key, dims, spread, bound, split=(), kind=jnp.bfloat16):
    entries = spread * jax.random.normal(own_key, dims, jnp.float32)
    if split:
        entries = entries * shard_levels(own_key, dims, split, -0.22, 0.18)
    return jnp.clip(entries, -bound, bound).astype(kind)


def setup_inputs(seed: int = 0, part: int = 0) -> dict:
    key_of = jax.random.split(jax.random.key(seed), 3)
    part_splits = jax.random.split(jax.random.fold_in(key_of[2], part), 3)
    traces = noise(part_splits[0], (CHANNELS, TIME_WINDOWS, WINDOW_SAMPLES), 1.0, 6.0, ((0, 16),))
    valid = draw_valid(jax.random.fold_in(jax.random.fold_in(key_of[2], part), 71), part)
    return {"traces": traces, "valid": valid}


epsilon = 1e-05

def forward_twiddles():
    samples = jnp.arange(WINDOW_SAMPLES, dtype=jnp.int32)
    bins = jnp.arange(FREQS, dtype=jnp.int32)
    phase = (samples[:, None] * bins[None, :] % WINDOW_SAMPLES).astype(jnp.float32) * (2.0 * math.pi / WINDOW_SAMPLES)
    table = jnp.concatenate([jnp.cos(phase), -jnp.sin(phase)], axis=1) / math.sqrt(WINDOW_SAMPLES)
    return table.astype(jnp.bfloat16)

def inverse_table():
    bins = jnp.arange(FREQS, dtype=jnp.int32)
    shifts = jnp.arange(LAGS, dtype=jnp.int32) - LAGS // 2
    phase = (bins[:, None] * shifts[None, :] % WINDOW_SAMPLES).astype(jnp.float32) * (2.0 * math.pi / WINDOW_SAMPLES)
    weight = jnp.where(bins == 0, 1.0, 2.0).astype(jnp.float32)[:, None] / math.sqrt(FREQS)
    table = jnp.concatenate([weight * jnp.cos(phase), -weight * jnp.sin(phase)], axis=0)
    return table.astype(jnp.bfloat16)

def whiten(traces, prior_sample, flags):
    pair_count = traces.shape[0]
    differenced_traces = (traces.astype(jnp.float32) - prior_sample.astype(jnp.float32)).astype(jnp.bfloat16)
    window_spectra = jnp.dot(differenced_traces.reshape(pair_count * TIME_WINDOWS, WINDOW_SAMPLES), forward_twiddles(), preferred_element_type=jnp.float32)
    window_spectra = window_spectra.reshape(pair_count, TIME_WINDOWS, 2 * FREQS)
    power = window_spectra[:, :, :FREQS] ** 2 + window_spectra[:, :, FREQS:] ** 2
    banded = lax.optimization_barrier(jnp.mean(power.reshape(pair_count, TIME_WINDOWS, FREQS // BAND, BAND), axis=-1))
    factor = jnp.repeat(lax.rsqrt(banded + epsilon), BAND, axis=-1) * flags[:, :, None]
    return (window_spectra * jnp.concatenate([factor, factor], axis=-1)).astype(jnp.bfloat16)

def correlate(own, partner, own_flags, partner_flags, inverse):
    highest = lax.Precision.HIGHEST
    own_real = own[:, :, :FREQS].astype(jnp.float32)
    own_imag = own[:, :, FREQS:].astype(jnp.float32)
    far_real = partner[:, :, :FREQS].astype(jnp.float32)
    far_imag = partner[:, :, FREQS:].astype(jnp.float32)
    real_part = jnp.einsum('iwf,jwf->fij', own_real, far_real, precision=highest) + jnp.einsum('iwf,jwf->fij', own_imag, far_imag, precision=highest)
    imag_part = jnp.einsum('iwf,jwf->fij', own_real, far_imag, precision=highest) - jnp.einsum('iwf,jwf->fij', own_imag, far_real, precision=highest)
    total = jnp.maximum(jnp.sum(own_flags * partner_flags), 1.0)
    stacked = (jnp.concatenate([real_part, imag_part], axis=0).reshape(2 * FREQS, CH * CH) / total).astype(jnp.bfloat16)
    result = lax.dot_general(stacked, inverse, (((0,), (0,)), ((), ())), preferred_element_type=jnp.float32)
    return result.reshape(CH, CH, LAGS).astype(jnp.bfloat16)

def reference(traces, valid):
    flags = valid.astype(jnp.float32)
    channel_flags = jnp.repeat(flags, CH, axis=0)
    prior_sample = jnp.concatenate([jnp.zeros((1, TIME_WINDOWS, WINDOW_SAMPLES), jnp.bfloat16), traces[:-1]], axis=0)
    whitened = whiten(traces, prior_sample, channel_flags).reshape(BLOCKS, CH, TIME_WINDOWS, 2 * FREQS)
    inverse = inverse_table()
    results = []
    for round_index in range(1, ROUNDS + 1):
        partner = jnp.roll(whitened, -round_index, axis=0)
        partner_flags = jnp.roll(flags, -round_index, axis=0)
        results.append(lax.map(lambda items: correlate(items[0], items[1], items[2], items[3], inverse), (whitened, partner, flags, partner_flags)))
    return jnp.stack(results, axis=0)
```

```python
import functools
import math

import jax
import jax.numpy as jnp
import ml_dtypes
import numpy as np
from jax import lax
from jax.experimental import pallas as pl
from jax.experimental.pallas import tpu as pltpu
from jax.sharding import PartitionSpec as P

LAGS = 512
BAND = 64
ROUNDS = 2
EPSILON = 1e-05
F8 = 8

f32 = jnp.float32
bf16 = jnp.bfloat16
VMEM = pltpu.VMEM


def forward_table(samples):
    freqs = samples // 2
    phase = (np.arange(samples)[:, None] * np.arange(freqs)[None, :]) % samples
    phase = phase * (2.0 * math.pi / samples)
    table = np.concatenate([np.cos(phase), -np.sin(phase)], axis=1) / math.sqrt(samples)
    return table.astype(np.float32).astype(ml_dtypes.bfloat16)


def inverse_table(samples):
    freqs = samples // 2
    bins = np.arange(freqs)
    shifts = np.arange(LAGS) - LAGS // 2
    phase = (bins[:, None] * shifts[None, :]) % samples
    phase = phase * (2.0 * math.pi / samples)
    weight = np.where(bins == 0, 1.0, 2.0)[:, None] / math.sqrt(freqs)
    table = np.concatenate([weight * np.cos(phase), -weight * np.sin(phase)], axis=0)
    return table.astype(np.float32).astype(ml_dtypes.bfloat16)


def dot(a, b):
    return jnp.dot(a, b, preferred_element_type=f32)


def dot_nt(a, b):
    return lax.dot_general(a, b, (((1,), (1,)), ((), ())), preferred_element_type=f32)


def left_kernel(trace_ref, prior_ref, flag_ref, forward_ref, left_ref, *, step):
    windows, samples = trace_ref.shape[1:]
    freqs = samples // 2
    k_own = 4 * windows
    lanes = k_own * F8
    per = step // 2
    s = pl.program_id(0)
    base = s * step
    before = trace_ref[pl.ds(jnp.maximum(base - 1, 0), 1)].astype(f32)
    before = jnp.where(s == 0, prior_ref[...].astype(f32), before)
    here = trace_ref[pl.ds(base, step)].astype(f32)
    diffed = here - jnp.concatenate([before, here[:-1]], axis=0)
    diffed = diffed.reshape(step * windows, samples).astype(bf16)
    spectra = dot(diffed, forward_ref[...])
    power = spectra[:, :freqs] ** 2 + spectra[:, freqs:] ** 2
    high = power.astype(bf16)
    low = (power - high.astype(f32)).astype(bf16)
    same = (
        lax.broadcasted_iota(jnp.int32, (freqs, freqs), 0) // BAND
        == lax.broadcasted_iota(jnp.int32, (freqs, freqs), 1) // BAND
    )
    mean = jnp.where(same, 1.0 / BAND, 0.0).astype(bf16)
    level = dot(high, mean) + dot(low, mean)
    factor = lax.rsqrt(level + EPSILON).reshape(step, windows, freqs) * flag_ref[...][None, :, :1]
    factor = factor.reshape(step * windows, freqs)
    real = (spectra[:, :freqs] * factor).reshape(per, 2 * windows, freqs)
    imag = (spectra[:, freqs:] * factor).reshape(per, 2 * windows, freqs)
    rows = jnp.concatenate([real, imag], axis=1).reshape(per * k_own, freqs)
    turned = rows.astype(bf16).T
    row = lax.broadcasted_iota(jnp.int32, (per * k_own, lanes), 0)
    col = lax.broadcasted_iota(jnp.int32, (per * k_own, lanes), 1)
    keep = (
        lax.broadcasted_iota(jnp.int32, (F8, lanes), 1) % F8
        == lax.broadcasted_iota(jnp.int32, (F8, lanes), 0)
    )[None]
    for pair in range(0, per, 2):
        both = []
        for q in range(2):
            spread = jnp.where(row == (pair + q) * k_own + col // F8, 1.0, 0.0).astype(bf16)
            wide = dot(turned, spread).reshape(freqs // F8, F8, lanes)
            both.append(jnp.where(keep, wide, 0.0))
        left_ref[:, pair * F8 : (pair + 2) * F8, :] = jnp.concatenate(both, axis=1).astype(bf16)


def left_side(traces, prior, flags, forward):
    channels, windows, samples = traces.shape
    freqs = samples // 2
    step = 16
    rows = channels // 2 * F8
    lanes = 4 * windows * F8
    return pl.pallas_call(
        functools.partial(left_kernel, step=step),
        grid=(channels // step,),
        in_specs=[
            pl.BlockSpec(traces.shape, lambda s: (0, 0, 0)),
            pl.BlockSpec(prior.shape, lambda s: (0, 0, 0)),
            pl.BlockSpec(flags.shape, lambda s: (0, 0)),
            pl.BlockSpec(forward.shape, lambda s: (0, 0)),
        ],
        out_specs=pl.BlockSpec((freqs // F8, step // 2 * F8, lanes), lambda s: (0, s, 0)),
        out_shape=jax.ShapeDtypeStruct((freqs // F8, rows, lanes), bf16),
        compiler_params=pltpu.CompilerParams(vmem_limit_bytes=28 * 2**20),
        cost_estimate=pl.CostEstimate(flops=4 * 10**9, bytes_accessed=12 * 2**20, transcendentals=0),
        name="left_side",
    )(traces, prior, flags, forward)


GROUPS_STEP = 8
PAIRS_STEP = 4


def pair_kernel(
    even_ref, trace_ref, other_ref, prior_ref, flag_ref, scale_ref, left_ref, forward_ref, inverse_ref, *rest,
    cross_steps,
):
    out_ref, spectra_ref, right_ref, cross_ref = rest[-4:]
    channels, windows, samples = trace_ref.shape
    freqs = samples // 2
    s = pl.program_id(0)
    half = channels

    @pl.when(s == 0)
    def _():
        here = trace_ref[...].astype(f32)
        if other_ref is not trace_ref:
            here = jnp.where(even_ref[0] == 1, other_ref[...].astype(f32), here)
        diffed = here - jnp.concatenate([prior_ref[...].astype(f32), here[:-1]], axis=0)
        turned = jnp.swapaxes(diffed, 0, 1).reshape(windows * channels, samples).astype(bf16)
        for n in range(2):
            width = windows * channels // 2
            spectra_ref[:, n * width : (n + 1) * width] = dot_nt(
                forward_ref[...], turned[n * width : (n + 1) * width]
            )

        def band(b, _):
            start = pl.multiple_of(b * BAND, BAND)
            groups = BAND // F8
            g = pl.multiple_of(b * groups, groups)
            lane = lax.broadcasted_iota(jnp.int32, (groups, F8, 2 * half), 2) < half
            for w2 in range(windows // 2):
                at = slice(w2 * 2 * half, (w2 + 1) * 2 * half)
                re = spectra_ref[pl.ds(start, BAND), at]
                im = spectra_ref[pl.ds(freqs + start, BAND), at]
                level = jnp.sum(re * re + im * im, axis=0, keepdims=True) * (1.0 / BAND)
                factor = lax.rsqrt(level + EPSILON) * flag_ref[:, at]
                tiles = []
                for part in (re, im):
                    t = (part * factor).reshape(groups, F8, 2 * half)
                    r = pltpu.roll(t.reshape(BAND, 2 * half), half, 1).reshape(groups, F8, 2 * half)
                    p0 = jnp.concatenate([jnp.where(lane, t, 0.0), jnp.where(lane, r, 0.0)], axis=1)
                    p1 = jnp.concatenate([jnp.where(lane, 0.0, r), jnp.where(lane, 0.0, t)], axis=1)
                    tiles.append((p0, p1))
                for p in range(2):
                    for q in range(2):
                        row = ((q * 2 + p) * windows + 2 * w2) * F8
                        rows = slice(row, row + 2 * F8)
                        first = tiles[q][p]
                        second = tiles[1][p] if q == 0 else -tiles[0][p]
                        right_ref[pl.ds(g, groups), rows, : 2 * half] = first.astype(bf16)
                        right_ref[pl.ds(g, groups), rows, 2 * half :] = second.astype(bf16)
            return 0

        lax.fori_loop(0, freqs // BAND, band, 0)

    @pl.when((s >= 1) & (s < 1 + cross_steps))
    def _():
        base = (s - 1) * GROUPS_STEP

        def two(k, _):
            outs = []
            for e in range(2):
                g = 2 * k + e
                product = dot(left_ref[g], right_ref[base + g])
                outs.append(product.reshape(channels // 2, F8, 4 * half))
            both = jnp.concatenate(outs, axis=1).astype(bf16)
            f = pl.multiple_of((base + 2 * k) * F8, 2 * F8)
            cross_ref[:, pl.ds(f, 2 * F8), :] = both[:, :, : 2 * half]
            cross_ref[:, pl.ds(freqs + f, 2 * F8), :] = both[:, :, 2 * half :]
            return 0

        lax.fori_loop(0, GROUPS_STEP // 2, two, 0)

    @pl.when(s >= 1 + cross_steps)
    def _():
        base = (s - 1 - cross_steps) * PAIRS_STEP
        scale = scale_ref[0]
        for k in range(0, PAIRS_STEP, 2):
            stacked = jnp.concatenate([cross_ref[base + k], cross_ref[base + k + 1]], axis=1)
            lags = dot(inverse_ref[...], stacked) * scale
            out_ref[0, 0, 2 * k : 2 * k + 4] = lags.astype(bf16).T.reshape(4, channels, LAGS)


def correlate(round_index, even, trace, other, prior, flag_lanes, scale, left, forward_t, inverse_t, out):
    channels, windows, samples = trace.shape
    freqs = samples // 2
    cross_steps = freqs // F8 // GROUPS_STEP
    lag_steps = channels // 2 // PAIRS_STEP
    whole = lambda x: pl.BlockSpec(x.shape, lambda s: (0,) * x.ndim)
    smem = pl.BlockSpec(memory_space=pltpu.SMEM)
    operands = [even, trace, other, prior, flag_lanes, scale, left, forward_t, inverse_t]
    in_specs = [
        smem,
        whole(trace),
        whole(other),
        whole(prior),
        whole(flag_lanes),
        smem,
        pl.BlockSpec(
            (GROUPS_STEP,) + left.shape[1:], lambda s: (jnp.clip(s - 1, 0, cross_steps - 1), 0, 0)
        ),
        whole(forward_t),
        whole(inverse_t),
    ]
    aliases = {}
    if out is not None:
        operands.append(out)
        in_specs.append(pl.BlockSpec(memory_space=pl.ANY))
        aliases = {len(operands) - 1: 0}
    return pl.pallas_call(
        functools.partial(pair_kernel, cross_steps=cross_steps),
        grid=(1 + cross_steps + lag_steps,),
        in_specs=in_specs,
        out_specs=pl.BlockSpec(
            (1, 1, 2 * PAIRS_STEP, channels, LAGS),
            lambda s: (round_index, 0, jnp.maximum(s - 1 - cross_steps, 0), 0, 0),
        ),
        out_shape=jax.ShapeDtypeStruct((ROUNDS, 1, channels, channels, LAGS), bf16),
        scratch_shapes=[
            VMEM((samples, windows * channels), f32),
            VMEM((freqs // F8, 4 * windows * F8, 4 * channels), bf16),
            VMEM((channels // 2, samples, 2 * channels), bf16),
        ],
        input_output_aliases=aliases,
        compiler_params=pltpu.CompilerParams(vmem_limit_bytes=44 * 2**20),
        cost_estimate=pl.CostEstimate(flops=7 * 10**9, bytes_accessed=20 * 2**20, transcendentals=0),
        name="correlate",
    )(*operands)


def shards(traces, valid):
    size = lax.axis_size("blk")
    index = lax.axis_index("blk")
    channels, windows, samples = traces.shape
    forward = forward_table(samples)
    forward_t = jnp.asarray(np.ascontiguousarray(forward.T))
    inverse_t = jnp.asarray(np.ascontiguousarray(inverse_table(samples).T))
    forward = jnp.asarray(forward)
    even = (index % 2 == 0).astype(jnp.int32).reshape(1)

    def permute(x, route):
        return lax.ppermute(x, "blk", route)

    ring = lambda d: [((i + d) % size, i) for i in range(size)]
    first = permute(traces, ring(1))
    second = permute(traces, [((i + 2) % size, i) for i in range(1, size, 2)])
    relay = permute(first, [(i + 1, i) for i in range(0, size, 2)])
    last = traces[channels - 1 :]
    before = permute(last, [(i, i + 1) for i in range(size - 1)])
    flags = valid.astype(bf16)
    partner_flags = [permute(flags, ring(r)) for r in range(1, ROUNDS + 1)]

    own = valid.astype(f32)
    left = left_side(traces, before, jnp.broadcast_to(own.reshape(windows, 1), (windows, 128)), forward)
    out = None
    prior = last
    partners = [(first, first), (second, relay)]
    for r in range(1, ROUNDS + 1):
        far = partner_flags[r - 1].astype(f32)
        scale = 1.0 / jnp.maximum(jnp.sum(own * far, axis=1), 1.0)
        lanes = jnp.repeat(far, channels, axis=1)
        edge = (index + r) % size == 0
        here = jnp.where(edge, jnp.zeros_like(prior), prior)
        trace, other = partners[r - 1]
        out = correlate(r - 1, even, trace, other, here, lanes, scale, left, forward_t, inverse_t, out)
        prior = trace[channels - 1 :]
    return out


def solution(mesh):
    return jax.shard_map(
        shards,
        mesh=mesh,
        in_specs=(P(("days", "blk"), None, None), P(("days", "blk"), None)),
        out_specs=P(None, ("days", "blk"), None, None, None),
        check_vma=False,
    )
```

```python
import functools
import math

import jax
import jax.numpy as jnp
import ml_dtypes
import numpy as np
from jax import lax
from jax.experimental import pallas as pl
from jax.experimental.pallas import tpu as pltpu
from jax.sharding import PartitionSpec as P

LAGS = 512
BAND = 64
ROUNDS = 2
EPSILON = 1e-05
F8 = 8

f32 = jnp.float32
bf16 = jnp.bfloat16
VMEM = pltpu.VMEM


def bin_order(freqs):
    bins = np.arange(freqs).reshape(-1, BAND)
    kinds = [bins[:, bins[0] % 4 == 0], bins[:, bins[0] % 4 == 2], bins[:, bins[0] % 2 == 1]]
    return np.concatenate(kinds, axis=1).reshape(-1)


def forward_table(samples):
    bins = bin_order(samples // 2)
    phase = (np.arange(samples)[:, None] * bins[None, :]) % samples
    phase = phase * (2.0 * math.pi / samples)
    table = np.concatenate([np.cos(phase), -np.sin(phase)], axis=1) / math.sqrt(samples)
    return table.astype(np.float32).astype(ml_dtypes.bfloat16)


def inverse_table(samples):
    freqs = samples // 2
    bins = np.arange(freqs)
    shifts = np.arange(LAGS) - LAGS // 2
    phase = (bins[:, None] * shifts[None, :]) % samples
    phase = phase * (2.0 * math.pi / samples)
    weight = np.where(bins == 0, 1.0, 2.0)[:, None] / math.sqrt(freqs)
    parts = [weight * np.cos(phase), -weight * np.sin(phase)]
    kinds = [bins % 4 == 0, bins % 4 == 2, bins % 2 == 1]
    table = np.concatenate([part[kind] for kind in kinds for part in parts], axis=0)
    return table.astype(np.float32).astype(ml_dtypes.bfloat16)


def dot(a, b):
    return jnp.dot(a, b, preferred_element_type=f32)


def dot_nt(a, b):
    return lax.dot_general(a, b, (((1,), (1,)), ((), ())), preferred_element_type=f32)


def dot_tn(a, b):
    return lax.dot_general(a, b, (((0,), (0,)), ((), ())), preferred_element_type=f32)


def left_kernel(trace_ref, prior_ref, forward_ref, left_ref, *, step):
    channels, windows, samples = trace_ref.shape
    channels -= 1
    freqs = samples // 2
    k_own = 4 * windows
    lanes = k_own * F8
    per = step // 2
    same = (
        lax.broadcasted_iota(jnp.int32, (freqs, freqs), 0) // BAND
        == lax.broadcasted_iota(jnp.int32, (freqs, freqs), 1) // BAND
    )
    mean = jnp.where(same, 1.0 / BAND, 0.0).astype(bf16)
    usable = trace_ref[channels, :, :freqs].astype(f32)
    row = lax.broadcasted_iota(jnp.int32, (per * k_own, lanes), 0)
    col = lax.broadcasted_iota(jnp.int32, (per * k_own, lanes), 1)
    keep = (
        lax.broadcasted_iota(jnp.int32, (F8, lanes), 1) % F8
        == lax.broadcasted_iota(jnp.int32, (F8, lanes), 0)
    )[None]

    def chunk(s, _):
        base = s * step
        before = trace_ref[pl.ds(jnp.maximum(base - 1, 0), 1)].astype(f32)
        before = jnp.where(s == 0, prior_ref[...].astype(f32), before)
        here = trace_ref[pl.ds(base, step)].astype(f32)
        diffed = here - jnp.concatenate([before, here[:-1]], axis=0)
        diffed = diffed.reshape(step * windows, samples).astype(bf16)
        spectra = dot(diffed, forward_ref[...])
        power = spectra[:, :freqs] ** 2 + spectra[:, freqs:] ** 2
        high = power.astype(bf16)
        low = (power - high.astype(f32)).astype(bf16)
        level = dot(high, mean) + dot(low, mean)
        factor = lax.rsqrt(level + EPSILON).reshape(step, windows, freqs) * usable[None]
        factor = factor.reshape(step * windows, freqs)
        real = (spectra[:, :freqs] * factor).reshape(per, 2 * windows, freqs)
        imag = (spectra[:, freqs:] * factor).reshape(per, 2 * windows, freqs)
        rows = jnp.concatenate([real, imag], axis=1).reshape(per * k_own, freqs)
        turned = rows.astype(bf16).T
        for pair in range(0, per, 2):
            both = []
            for q in range(2):
                spread = jnp.where(row == (pair + q) * k_own + col // F8, 1.0, 0.0).astype(bf16)
                wide = dot(turned, spread).reshape(freqs // F8, F8, lanes)
                both.append(jnp.where(keep, wide, 0.0))
            at = pl.multiple_of((s * per + pair) * F8, 2 * F8)
            left_ref[:, pl.ds(at, 2 * F8), :] = jnp.concatenate(both, axis=1).astype(bf16)
        return 0

    lax.fori_loop(0, channels // step, chunk, 0)


SMEM_SPEC = pl.BlockSpec(memory_space=pltpu.SMEM)
VMEM_SPEC = pl.BlockSpec(memory_space=pltpu.VMEM)


def left_side(traces, prior, forward):
    channels, windows, samples = traces.shape
    channels -= 1
    freqs = samples // 2
    return pl.pallas_call(
        functools.partial(left_kernel, step=16),
        in_specs=[VMEM_SPEC] * 3,
        out_specs=VMEM_SPEC,
        out_shape=jax.ShapeDtypeStruct((freqs // F8, channels // 2 * F8, 4 * windows * F8), bf16),
        compiler_params=pltpu.CompilerParams(vmem_limit_bytes=28 * 2**20),
        cost_estimate=pl.CostEstimate(flops=4 * 10**9, bytes_accessed=12 * 2**20, transcendentals=0),
        name="left_side",
    )(traces, prior, forward)


def pair_kernel(
    trace_ref, other_ref, own_ref, prior_ref, left_ref, forward_ref, inverse_ref, *rest,
    round_index,
):
    out_ref, spectra_ref, right_ref, cross_ref, lag_ref, sems = rest[-6:]
    channels, windows, samples = trace_ref.shape
    channels -= 1
    freqs = samples // 2
    half = channels
    size = lax.axis_size("blk")
    index = lax.axis_index("blk")

    here = trace_ref[...].astype(f32)
    if other_ref is not None:
        here = jnp.where(index % 2 == 0, other_ref[...].astype(f32), here)
    far_flags, here = here[channels], here[:channels]
    edge = lax.rem(index + round_index, size) == 0
    before = jnp.where(edge, 0.0, prior_ref[channels - 1 : channels].astype(f32))
    diffed = here - jnp.concatenate([before, here[:-1]], axis=0)
    turned = jnp.swapaxes(diffed, 0, 1).reshape(windows * channels, samples).astype(bf16)
    for n in range(2):
        width = windows * channels // 2
        spectra_ref[:, n * width : (n + 1) * width] = dot_nt(
            forward_ref[...], turned[n * width : (n + 1) * width]
        )

    first_half = lax.broadcasted_iota(jnp.int32, (1, 2 * half), 1) < half
    usable = [
        jnp.where(first_half, far_flags[w : w + 1, : 2 * half], far_flags[w + 1 : w + 2, : 2 * half])
        for w in range(0, windows, 2)
    ]

    groups = BAND // F8
    lane = lax.broadcasted_iota(jnp.int32, (groups, F8, 2 * half), 2) < half

    def whiten(b):
        start, g = b * BAND, b * groups
        for w2 in range(windows // 2):
            at = slice(w2 * 2 * half, (w2 + 1) * 2 * half)
            re = spectra_ref[start : start + BAND, at]
            im = spectra_ref[freqs + start : freqs + start + BAND, at]
            level = jnp.sum(re * re + im * im, axis=0, keepdims=True) * (1.0 / BAND)
            factor = lax.rsqrt(level + EPSILON) * usable[w2]
            tiles = []
            for part in (re, im):
                t = (part * factor).reshape(groups, F8, 2 * half)
                r = pltpu.roll(t.reshape(BAND, 2 * half), half, 1).reshape(groups, F8, 2 * half)
                p0 = jnp.concatenate([jnp.where(lane, t, 0.0), jnp.where(lane, r, 0.0)], axis=1)
                p1 = jnp.concatenate([jnp.where(lane, 0.0, r), jnp.where(lane, 0.0, t)], axis=1)
                tiles.append((p0, p1))
            for p in range(2):
                for q in range(2):
                    row = ((q * 2 + p) * windows + 2 * w2) * F8
                    rows = slice(row, row + 2 * F8)
                    first = tiles[q][p]
                    second = tiles[1][p] if q == 0 else -tiles[0][p]
                    right_ref[g : g + groups, rows, : 2 * half] = first.astype(bf16)
                    right_ref[g : g + groups, rows, 2 * half :] = second.astype(bf16)

    def cross(b):
        bands = freqs // BAND
        quarter = BAND // 4
        for pair in range(groups // 2):
            outs = []
            for e in range(2):
                g = b * groups + 2 * pair + e
                product = dot(left_ref[g], right_ref[g])
                outs.append(product.reshape(channels // 2, F8, 4 * half))
            both = jnp.concatenate(outs, axis=1).astype(bf16)
            kind = min(pair, 2)
            count = 1 if kind < 2 else 2
            row = 2 * kind * bands * quarter + (b * count + pair - kind) * quarter
            cross_ref[:, row : row + quarter, :] = both[:, :, : 2 * half]
            row += count * bands * quarter
            cross_ref[:, row : row + quarter, :] = both[:, :, 2 * half :]

    whiten(0)
    for b in range(freqs // BAND):
        if b + 1 < freqs // BAND:
            whiten(b + 1)
        cross(b)

    both_flags = own_ref[channels, :, :LAGS].astype(f32) * far_flags[:, :LAGS]
    scale = 1.0 / jnp.maximum(jnp.sum(both_flags, axis=0, keepdims=True), 1.0)

    group = 4

    def copy(k):
        at = pl.ds(k * 2 * group, 2 * group)
        return pltpu.make_async_copy(lag_ref.at[at], out_ref.at[round_index - 1, 0, at], sems.at[k])

    copies = channels // 2 // group
    quarter = samples // 4
    near = LAGS // 2

    def lags(k, _):
        for u in range(LAG_UNROLL):
            n = k * LAG_UNROLL + u
            stacked = jnp.concatenate([cross_ref[n * group + e] for e in range(group)], axis=1)
            zero = dot_tn(stacked[:quarter], inverse_ref[:quarter, :near])
            two = dot_tn(stacked[quarter : 2 * quarter], inverse_ref[quarter : 2 * quarter, :near])
            odd = dot_tn(stacked[2 * quarter :], inverse_ref[2 * quarter :, :])
            result = jnp.concatenate([zero + two + odd[:, :near], zero - two + odd[:, near:]], axis=1) * scale
            lag_ref[pl.ds(n * 2 * group, 2 * group)] = result.astype(bf16).reshape(2 * group, channels, LAGS)
            copy(n).start()
        return 0

    lax.fori_loop(0, copies // LAG_UNROLL, lags, 0)

    def finish(k, _):
        copy(k).wait()
        return 0

    lax.fori_loop(0, copies, finish, 0)


LAG_UNROLL = 4


def correlate(round_index, trace, other, own, prior, left, forward_t, inverse, out):
    channels, windows, samples = trace.shape
    channels -= 1
    freqs = samples // 2
    operands = [trace] + ([other] if other is not None else []) + [own]
    operands += ([prior] if prior is not own else []) + [left, forward_t, inverse]
    in_specs = [VMEM_SPEC] * len(operands)
    aliases = {}
    if out is not None:
        operands.append(out)
        in_specs.append(pl.BlockSpec(memory_space=pl.ANY))
        aliases = {len(operands) - 1: 0}

    def kernel(trace_ref, *refs):
        refs = list(refs)
        other_ref = refs.pop(0) if other is not None else None
        own_ref = refs.pop(0)
        prior_ref = refs.pop(0) if prior is not own else own_ref
        pair_kernel(trace_ref, other_ref, own_ref, prior_ref, *refs, round_index=round_index)

    return pl.pallas_call(
        kernel,
        in_specs=in_specs,
        out_specs=pl.BlockSpec(memory_space=pl.ANY),
        out_shape=jax.ShapeDtypeStruct((ROUNDS, 1, channels, channels, LAGS), bf16),
        scratch_shapes=[
            VMEM((samples, windows * channels), f32),
            VMEM((freqs // F8, 4 * windows * F8, 4 * channels), bf16),
            VMEM((channels // 2, samples, 2 * channels), bf16),
            VMEM((channels, channels, LAGS), bf16),
            pltpu.SemaphoreType.DMA((channels // 8,)),
        ],
        input_output_aliases=aliases,
        compiler_params=pltpu.CompilerParams(vmem_limit_bytes=32 * 2**20),
        cost_estimate=pl.CostEstimate(flops=7 * 10**9, bytes_accessed=20 * 2**20, transcendentals=0),
        name="correlate",
    )(*operands)


def shards(traces, valid):
    size = lax.axis_size("blk")
    channels, windows, samples = traces.shape
    forward = forward_table(samples)
    forward_t = jnp.asarray(np.ascontiguousarray(forward.T))
    inverse = jnp.asarray(inverse_table(samples))
    forward = jnp.asarray(forward)

    def permute(x, route):
        return lax.ppermute(x, "blk", route)

    ring = lambda d: [((i + d) % size, i) for i in range(size)]
    before = permute(traces[channels - 1 :], [(i, i + 1) for i in range(size - 1)])
    flag_row = jnp.broadcast_to(valid.astype(bf16)[:, :, None], (1, windows, samples))
    block = jnp.concatenate([traces, flag_row], axis=0)
    block, before = lax.optimization_barrier((block, before))
    first = permute(block, ring(1))
    left = left_side(block, before, forward)
    left, sent = lax.optimization_barrier((left, block))
    second = permute(sent, [((i + 2) % size, i) for i in range(1, size, 2)])
    first, left = lax.optimization_barrier((first, left))
    relay = permute(first, [(i + 1, i) for i in range(0, size, 2)])

    out = correlate(1, first, None, block, block, left, forward_t, inverse, None)
    return correlate(2, second, relay, block, first, left, forward_t, inverse, out)


def solution(mesh):
    return jax.shard_map(
        shards,
        mesh=mesh,
        in_specs=(P(("days", "blk"), None, None), P(("days", "blk"), None)),
        out_specs=P(None, ("days", "blk"), None, None, None),
        check_vma=False,
    )
```

```python
import functools
import math

import jax
import jax.numpy as jnp
import ml_dtypes
import numpy as np
from jax import lax
from jax.experimental import pallas as pl
from jax.experimental.pallas import tpu as pltpu
from jax.sharding import PartitionSpec as P

CH = 64
LAGS = 512
BAND = 64
ROUNDS = 2
EPSILON = 1e-05
F8 = 8

f32 = jnp.float32
bf16 = jnp.bfloat16
VMEM = pltpu.VMEM


def bin_order(freqs):
    bins = np.arange(freqs).reshape(-1, BAND)
    kinds = [bins[:, bins[0] % 4 == 0], bins[:, bins[0] % 4 == 2], bins[:, bins[0] % 2 == 1]]
    return np.concatenate(kinds, axis=1).reshape(-1)


def forward_table(samples):
    bins = bin_order(samples // 2)
    phase = (np.arange(samples)[:, None] * bins[None, :]) % samples
    phase = phase * (2.0 * math.pi / samples)
    table = np.concatenate([np.cos(phase), -np.sin(phase)], axis=1) / math.sqrt(samples)
    return table.astype(np.float32).astype(ml_dtypes.bfloat16)


def inverse_table(samples):
    freqs = samples // 2
    bins = np.arange(freqs)
    shifts = np.arange(LAGS) - LAGS // 2
    phase = (bins[:, None] * shifts[None, :]) % samples
    phase = phase * (2.0 * math.pi / samples)
    weight = np.where(bins == 0, 1.0, 2.0)[:, None] / math.sqrt(freqs)
    parts = [weight * np.cos(phase), -weight * np.sin(phase)]
    kinds = [bins % 4 == 0, bins % 4 == 2, bins % 2 == 1]
    table = np.concatenate([part[kind] for kind in kinds for part in parts], axis=0)
    return table.astype(np.float32).astype(ml_dtypes.bfloat16)


def dot(a, b):
    return jnp.dot(a, b, preferred_element_type=f32)


def dot_nt(a, b):
    return lax.dot_general(a, b, (((1,), (1,)), ((), ())), preferred_element_type=f32)


def dot_tn(a, b):
    return lax.dot_general(a, b, (((0,), (0,)), ((), ())), preferred_element_type=f32)


SMEM_SPEC = pl.BlockSpec(memory_space=pltpu.SMEM)
VMEM_SPEC = pl.BlockSpec(memory_space=pltpu.VMEM)
EXTRA = 16


def early_windows(windows):
    return windows * 3 // 4


def block_kernel(flag_ref, trace_ref, early_ref, late_ref, held_ref, sems, *, step):
    channels, windows, samples = trace_ref.shape
    early = early_windows(windows)

    def copy(c):
        at = pl.ds(c * step, step)
        return pltpu.make_async_copy(trace_ref.at[at], held_ref.at[at], sems.at[c])

    for c in range(channels // step):
        copy(c).start()
    last = None
    for c in range(channels // step):
        copy(c).wait()
        here = held_ref[c * step : (c + 1) * step].astype(f32)
        before = jnp.zeros_like(here[:1]) if last is None else last
        diffed = here - jnp.concatenate([before, here[:-1]], axis=0)
        last = here[step - 1 :]
        turned = jnp.swapaxes(diffed, 0, 1).astype(bf16)
        for w in range(windows):
            row = (w if w < early else w - early) * channels + c * step
            (early_ref if w < early else late_ref)[row : row + step] = turned[w]
    window = lax.broadcasted_iota(jnp.int32, (windows, samples), 0)
    flags = jnp.zeros((windows, samples), f32)
    for w in range(windows):
        flags = jnp.where(window == w, flag_ref[0, w].astype(f32), flags)
    early_ref[early * channels :] = jnp.concatenate([last[0], flags], axis=0).astype(bf16)


def travelling(flags, traces):
    channels, windows, samples = traces.shape
    step = 16
    early = early_windows(windows)
    return pl.pallas_call(
        functools.partial(block_kernel, step=step),
        in_specs=[SMEM_SPEC, pl.BlockSpec(memory_space=pl.ANY)],
        out_specs=(VMEM_SPEC,) * 2,
        out_shape=(
            jax.ShapeDtypeStruct((early * channels + EXTRA, samples), bf16),
            jax.ShapeDtypeStruct(((windows - early) * channels, samples), bf16),
        ),
        scratch_shapes=[
            VMEM(traces.shape, bf16),
            pltpu.SemaphoreType.DMA((channels // step,)),
        ],
        compiler_params=pltpu.CompilerParams(vmem_limit_bytes=52 * 2**20),
        cost_estimate=pl.CostEstimate(flops=10**10, bytes_accessed=2 * 2**20, transcendentals=0),
        name="travelling",
    )(flags, traces)


def extra_rows(piece_ref):
    extra = piece_ref[piece_ref.shape[0] - EXTRA :].astype(f32)
    return extra[: EXTRA // 2], extra[EXTRA // 2 :]


def less_before(tile, before):
    first = lax.broadcasted_iota(jnp.int32, tile.shape, 0) == 0
    tile = tile.astype(f32)
    return jnp.where(first, tile - before, tile).astype(bf16)


def left_kernel(early_ref, late_ref, before_ref, forward_ref, left_ref, block_ref, *, step, windows):
    early = early_windows(windows)
    channels = late_ref.shape[0] // (windows - early)
    samples = late_ref.shape[1]
    freqs = samples // 2
    k_own = 4 * windows
    lanes = k_own * F8
    per = step // 2
    same = (
        lax.broadcasted_iota(jnp.int32, (freqs, freqs), 0) // BAND
        == lax.broadcasted_iota(jnp.int32, (freqs, freqs), 1) // BAND
    )
    mean = jnp.where(same, 1.0 / BAND, 0.0).astype(bf16)
    before = before_ref[0].astype(f32)
    block_ref[: early * channels] = early_ref[: early * channels]
    block_ref[early * channels : windows * channels] = late_ref[...]
    block_ref[windows * channels :] = early_ref[early * channels :]
    _, flags = extra_rows(early_ref)
    usable = jnp.concatenate(
        [jnp.broadcast_to(flags[w : w + 1, :freqs], (step, freqs)) for w in range(windows)],
        axis=0,
    )
    row = lax.broadcasted_iota(jnp.int32, (2 * step * windows, lanes), 0)
    k = lax.broadcasted_iota(jnp.int32, (2 * step * windows, lanes), 1) // F8
    place = k // 4 % 2 * (step * windows) + (k // 8 * 2 + k % 2) * step + k // 2 % 2
    keep = (
        lax.broadcasted_iota(jnp.int32, (F8, lanes), 1) % F8
        == lax.broadcasted_iota(jnp.int32, (F8, lanes), 0)
    )[None]

    def chunk(s, _):
        base = s * step
        tiles = []
        for w in range(windows):
            at = (w if w < early else w - early) * channels
            tile = (early_ref if w < early else late_ref)[pl.ds(pl.multiple_of(at + base, step), step)]
            tiles.append(less_before(tile, jnp.where(s == 0, before[w : w + 1], 0.0)))
        spectra = dot_nt(jnp.concatenate(tiles, axis=0), forward_ref[...])
        power = spectra[:, :freqs] ** 2 + spectra[:, freqs:] ** 2
        high = power.astype(bf16)
        low = (power - high.astype(f32)).astype(bf16)
        level = dot(high, mean) + dot(low, mean)
        factor = lax.rsqrt(level + EPSILON) * usable
        parts = jnp.concatenate([spectra[:, :freqs] * factor, spectra[:, freqs:] * factor], axis=0)
        turned = parts.astype(bf16).T
        for pair in range(0, per, 2):
            both = []
            for q in range(2):
                spread = jnp.where(row == place + 2 * (pair + q), 1.0, 0.0).astype(bf16)
                wide = dot(turned, spread).reshape(freqs // F8, F8, lanes)
                both.append(jnp.where(keep, wide, 0.0))
            at = pl.multiple_of((s * per + pair) * F8, 2 * F8)
            left_ref[:, pl.ds(at, 2 * F8), :] = jnp.concatenate(both, axis=1).astype(bf16)
        return 0

    lax.fori_loop(0, channels // step, chunk, 0)


def left_side(early, late, before, forward, windows):
    samples = late.shape[1]
    channels = late.shape[0] // (windows - early_windows(windows))
    freqs = samples // 2
    return pl.pallas_call(
        functools.partial(left_kernel, step=16, windows=windows),
        in_specs=[VMEM_SPEC] * 4,
        out_specs=(VMEM_SPEC,) * 2,
        out_shape=(
            jax.ShapeDtypeStruct((freqs // F8, channels // 2 * F8, 4 * windows * F8), bf16),
            jax.ShapeDtypeStruct((windows * channels + EXTRA, samples), bf16),
        ),
        compiler_params=pltpu.CompilerParams(vmem_limit_bytes=28 * 2**20),
        cost_estimate=pl.CostEstimate(flops=4 * 10**9, bytes_accessed=12 * 2**20, transcendentals=0),
        name="left_side",
    )(early, late, before, forward)


def placed(index, even_rows, odd_rows):
    return odd_rows if even_rows is None else jnp.where(index % 2 == 0, even_rows, odd_rows)


def differences(rows, before, channels):
    tiles = []
    for w in range(rows.shape[0] // channels):
        tiles.append(less_before(rows[w * channels : w * channels + 16], before[w : w + 1]))
        tiles.append(rows[w * channels + 16 : (w + 1) * channels])
    return jnp.concatenate(tiles, axis=0)


def before_first(prior_ref, index, round_index):
    last, _ = extra_rows(prior_ref)
    return jnp.where(lax.rem(index + round_index, lax.axis_size("blk")) == 0, 0.0, last)


def window_pair_flags(flags, windows, half):
    first_half = lax.broadcasted_iota(jnp.int32, (1, 2 * half), 1) < half
    return [
        jnp.where(first_half, flags[w : w + 1, : 2 * half], flags[w + 1 : w + 2, : 2 * half])
        for w in range(0, windows, 2)
    ]


def whitened_pair(spectra_ref, band, at, usable):
    freqs = spectra_ref.shape[0] // 2
    start = band * BAND
    re = spectra_ref[start : start + BAND, at]
    im = spectra_ref[freqs + start : freqs + start + BAND, at]
    level = jnp.sum(re * re + im * im, axis=0, keepdims=True) * (1.0 / BAND)
    factor = lax.rsqrt(level + EPSILON) * usable
    return re * factor, im * factor


def right_kernel(odd_refs, even_refs, odd_flag_ref, even_flag_ref, prior_ref, forward_ref, right_ref, spectra_ref, *,
                 round_index, skip):
    samples = prior_ref.shape[1]
    freqs = samples // 2
    pairs = right_ref.shape[0]
    half = spectra_ref.shape[1] // (2 * pairs)
    index = lax.axis_index("blk")

    def rows_of(refs):
        rows = jnp.concatenate([ref[: ref.shape[0] // half * half] for ref in refs], axis=0)
        return rows[: 2 * pairs * half]

    here = placed(index, None if even_refs is None else rows_of(even_refs), rows_of(odd_refs))
    _, flags = extra_rows(odd_flag_ref)
    if even_flag_ref is not None:
        flags = placed(index, extra_rows(even_flag_ref)[1], flags)
    before = before_first(prior_ref, index, round_index)[skip:]
    spectra_ref[...] = dot_nt(forward_ref[...], differences(here, before, half))
    usable = window_pair_flags(flags[skip:], 2 * pairs, half)
    groups = BAND // F8
    lane = lax.broadcasted_iota(jnp.int32, (groups, F8, 2 * half), 2) < half
    for b in range(freqs // BAND):
        g = b * groups
        for w2 in range(pairs):
            tiles = []
            at = slice(w2 * 2 * half, (w2 + 1) * 2 * half)
            for part in whitened_pair(spectra_ref, b, at, usable[w2]):
                t = part.reshape(groups, F8, 2 * half)
                r = pltpu.roll(part, half, 1).reshape(groups, F8, 2 * half)
                p0 = jnp.concatenate([jnp.where(lane, t, 0.0), jnp.where(lane, r, 0.0)], axis=1)
                p1 = jnp.concatenate([jnp.where(lane, 0.0, r), jnp.where(lane, 0.0, t)], axis=1)
                tiles.append((p0.astype(bf16), p1.astype(bf16)))
            for p in range(2):
                for q in range(2):
                    rows = slice((2 * q + p) * 2 * F8, (2 * q + p + 1) * 2 * F8)
                    right_ref[w2, g : g + groups, rows, : 2 * half] = tiles[q][p]
                    right_ref[w2, g : g + groups, rows, 2 * half :] = tiles[1][p] if q == 0 else -tiles[0][p]


def right_side(round_index, mine, skip, odd, even, prior, forward_t):
    samples = prior.shape[1]
    freqs = samples // 2
    operands, places = [], []
    for array in odd + (even or []) + [prior, forward_t]:
        if not any(array is other for other in operands):
            operands.append(array)
        places.append(next(i for i, other in enumerate(operands) if other is array))
    channels = CH

    def kernel(*refs):
        named = [refs[i] for i in places]
        odd_refs = [named.pop(0) for _ in odd]
        even_refs = [named.pop(0) for _ in even or []]
        right_kernel(odd_refs[:-1], even_refs[:-1] or None, odd_refs[-1], even_refs[-1] if even else None, *named,
                     *refs[len(operands) :], round_index=round_index, skip=skip)

    return pl.pallas_call(
        kernel,
        in_specs=[VMEM_SPEC] * len(operands),
        out_specs=VMEM_SPEC,
        out_shape=jax.ShapeDtypeStruct((mine // 2, freqs // F8, 8 * F8, 4 * channels), bf16),
        scratch_shapes=[VMEM((samples, mine * channels), f32)],
        compiler_params=pltpu.CompilerParams(vmem_limit_bytes=20 * 2**20),
        cost_estimate=pl.CostEstimate(flops=2 * 10**9, bytes_accessed=5 * 2**20, transcendentals=0),
        name="right_side",
    )(*operands)


def pair_kernel(
    odd_early_ref, even_early_ref, own_ref, left_ref, right_refs, inverse_ref, *rest, round_index
):
    out_ref, cross_ref, lag_ref, sems = rest[-4:]
    channels = right_refs[0].shape[3] // 4
    samples = inverse_ref.shape[0]
    freqs = samples // 2
    half = channels
    groups = BAND // F8
    index = lax.axis_index("blk")
    _, far_flags = extra_rows(odd_early_ref)
    if even_early_ref is not None:
        far_flags = placed(index, extra_rows(even_early_ref)[1], far_flags)
    _, own_flags = extra_rows(own_ref)

    def cross(b):
        bands = freqs // BAND
        quarter = BAND // 4
        for pair in range(groups // 2):
            outs = []
            for e in range(2):
                g = b * groups + 2 * pair + e
                right = [ref[w2, g] for ref in right_refs for w2 in range(ref.shape[0])]
                product = dot(left_ref[g], jnp.concatenate(right, axis=0))
                outs.append(product.reshape(channels // 2, F8, 4 * half))
            both = jnp.concatenate(outs, axis=1).astype(bf16)
            kind = min(pair, 2)
            count = 1 if kind < 2 else 2
            row = 2 * kind * bands * quarter + (b * count + pair - kind) * quarter
            cross_ref[:, row : row + quarter, :] = both[:, :, : 2 * half]
            row += count * bands * quarter
            cross_ref[:, row : row + quarter, :] = both[:, :, 2 * half :]

    for b in range(freqs // BAND):
        cross(b)

    both_flags = own_flags[:, :LAGS] * far_flags[:, :LAGS]
    scale = 1.0 / jnp.maximum(jnp.sum(both_flags, axis=0, keepdims=True), 1.0)

    group = 4

    def copy(k):
        at = pl.ds(k * 2 * group, 2 * group)
        return pltpu.make_async_copy(lag_ref.at[at], out_ref.at[round_index - 1, 0, at], sems.at[k])

    copies = channels // 2 // group
    quarter = samples // 4
    near = LAGS // 2

    def lags(k, _):
        for u in range(LAG_UNROLL):
            n = k * LAG_UNROLL + u
            stacked = jnp.concatenate([cross_ref[n * group + e] for e in range(group)], axis=1)
            zero = dot_tn(stacked[:quarter], inverse_ref[:quarter, :near])
            two = dot_tn(stacked[quarter : 2 * quarter], inverse_ref[quarter : 2 * quarter, :near])
            odd = dot_tn(stacked[2 * quarter :], inverse_ref[2 * quarter :, :])
            result = jnp.concatenate([zero + two + odd[:, :near], zero - two + odd[:, near:]], axis=1) * scale
            lag_ref[pl.ds(n * 2 * group, 2 * group)] = result.astype(bf16).reshape(2 * group, channels, LAGS)
            copy(n).start()
        return 0

    lax.fori_loop(0, copies // LAG_UNROLL, lags, 0)

    def finish(k, _):
        copy(k).wait()
        return 0

    lax.fori_loop(0, copies, finish, 0)


LAG_UNROLL = 8


def correlate(round_index, odd, even, own, left, rights, inverse, out):
    channels = rights[0].shape[3] // 4
    samples = inverse.shape[0]
    operands = [odd] + ([even] if even is not None else []) + [own, left, *rights, inverse]
    in_specs = [VMEM_SPEC] * len(operands)
    aliases = {}
    if out is not None:
        operands.append(out)
        in_specs.append(pl.BlockSpec(memory_space=pl.ANY))
        aliases = {len(operands) - 1: 0}

    def kernel(odd_ref, *refs):
        refs = list(refs)
        even_ref = refs.pop(0) if even is not None else None
        own_ref, left_ref = refs.pop(0), refs.pop(0)
        right_refs = [refs.pop(0) for _ in rights]
        pair_kernel(odd_ref, even_ref, own_ref, left_ref, right_refs, *refs, round_index=round_index)

    return pl.pallas_call(
        kernel,
        in_specs=in_specs,
        out_specs=pl.BlockSpec(memory_space=pl.ANY),
        out_shape=jax.ShapeDtypeStruct((ROUNDS, 1, channels, channels, LAGS), bf16),
        scratch_shapes=[
            VMEM((channels // 2, samples, 2 * channels), bf16),
            VMEM((channels, channels, LAGS), bf16),
            pltpu.SemaphoreType.DMA((channels // 8,)),
        ],
        input_output_aliases=aliases,
        compiler_params=pltpu.CompilerParams(vmem_limit_bytes=20 * 2**20),
        cost_estimate=pl.CostEstimate(flops=7 * 10**9, bytes_accessed=20 * 2**20, transcendentals=0),
        name="correlate",
    )(*operands)


def shards(traces, valid):
    size = lax.axis_size("blk")
    channels, windows, samples = traces.shape
    forward_t = jnp.asarray(np.ascontiguousarray(forward_table(samples).T))
    inverse = jnp.asarray(inverse_table(samples))

    def permute(x, route):
        return lax.ppermute(x, "blk", route)

    ring = lambda d: [((i + d) % size, i) for i in range(size)]
    before = permute(traces[channels - 1 :], [(i, i + 1) for i in range(size - 1)])
    early, late = travelling(valid, traces)
    early, late, before = lax.optimization_barrier((early, late, before))
    to_odd = [((i + 2) % size, i) for i in range(1, size, 2)]
    swap = [(i ^ 1, i) for i in range(size)]
    first_early = permute(early, ring(1))
    first_late = permute(late, ring(1))
    left, block = left_side(early, late, before, forward_t, windows)
    second = permute(block, to_odd)
    first_early, left = lax.optimization_barrier((first_early, left))
    relay_early = permute(first_early, swap)
    count = early_windows(windows)
    rights = [right_side(1, count, 0, [first_early, first_early], None, early, forward_t)]
    first_late, rights = lax.optimization_barrier((first_late, rights))
    relay_late = permute(first_late, swap)
    rights += [right_side(1, windows - count, count, [first_late, first_early], None, early, forward_t)]
    out = correlate(1, first_early, None, early, left, rights, inverse, None)

    relay = [relay_early, relay_late, relay_early]
    rights = [right_side(2, windows, 0, [second, second], relay, first_early, forward_t)]
    return correlate(2, second, relay_early, early, left, rights, inverse, out)


def solution(mesh):
    return jax.shard_map(
        shards,
        mesh=mesh,
        in_specs=(P(("days", "blk"), None, None), P(("days", "blk"), None)),
        out_specs=P(None, ("days", "blk"), None, None, None),
        check_vma=False,
    )
```

```python
import functools
import math

import jax
import jax.numpy as jnp
import ml_dtypes
import numpy as np
from jax import lax
from jax.experimental import pallas as pl
from jax.experimental.pallas import tpu as pltpu
from jax.sharding import PartitionSpec as P

CH = 64
LAGS = 512
BAND = 64
ROUNDS = 2
EPSILON = 1e-05
F8 = 8

f32 = jnp.float32
bf16 = jnp.bfloat16
VMEM = pltpu.VMEM


def bin_order(freqs):
    bins = np.arange(freqs).reshape(-1, BAND)
    kinds = [bins[:, bins[0] % 4 == 0], bins[:, bins[0] % 4 == 2], bins[:, bins[0] % 2 == 1]]
    return np.concatenate(kinds, axis=1).reshape(-1)


def forward_table(samples):
    bins = bin_order(samples // 2)
    phase = (np.arange(samples)[:, None] * bins[None, :]) % samples
    phase = phase * (2.0 * math.pi / samples)
    table = np.concatenate([np.cos(phase), -np.sin(phase)], axis=1) / math.sqrt(samples)
    return table.astype(np.float32).astype(ml_dtypes.bfloat16)


def inverse_table(samples):
    freqs = samples // 2
    bins = np.arange(freqs)
    shifts = np.arange(LAGS) - LAGS // 2
    phase = (bins[:, None] * shifts[None, :]) % samples
    phase = phase * (2.0 * math.pi / samples)
    weight = np.where(bins == 0, 1.0, 2.0)[:, None] / math.sqrt(freqs)
    parts = [weight * np.cos(phase), -weight * np.sin(phase)]
    kinds = [bins % 4 == 0, bins % 4 == 2, bins % 2 == 1]
    table = np.concatenate([part[kind] for kind in kinds for part in parts], axis=0)
    return table.astype(np.float32).astype(ml_dtypes.bfloat16)


def dot(a, b):
    return jnp.dot(a, b, preferred_element_type=f32)


def dot_nt(a, b):
    return lax.dot_general(a, b, (((1,), (1,)), ((), ())), preferred_element_type=f32)


def dot_tn(a, b):
    return lax.dot_general(a, b, (((0,), (0,)), ((), ())), preferred_element_type=f32)


SMEM_SPEC = pl.BlockSpec(memory_space=pltpu.SMEM)
VMEM_SPEC = pl.BlockSpec(memory_space=pltpu.VMEM)
EXTRA = 16


def early_windows(windows):
    return windows * 3 // 4


def block_kernel(flag_ref, trace_ref, early_ref, late_ref, held_ref, held_flag_ref, sems, flag_sem, *, step):
    channels, windows, samples = trace_ref.shape
    early = early_windows(windows)

    def copy(c):
        at = pl.ds(c * step, step)
        return pltpu.make_async_copy(trace_ref.at[at], held_ref.at[at], sems.at[c])

    flag_copy = pltpu.make_async_copy(flag_ref, held_flag_ref, flag_sem)
    for c in range(channels // step):
        copy(c).start()
    flag_copy.start()
    last = None
    for c in range(channels // step):
        copy(c).wait()
        here = held_ref[c * step : (c + 1) * step].astype(f32)
        before = jnp.zeros_like(here[:1]) if last is None else last
        diffed = here - jnp.concatenate([before, here[:-1]], axis=0)
        last = here[step - 1 :]
        turned = jnp.swapaxes(diffed, 0, 1).astype(bf16)
        for w in range(windows):
            row = (w if w < early else w - early) * channels + c * step
            (early_ref if w < early else late_ref)[row : row + step] = turned[w]
    flag_copy.wait()
    window = lax.broadcasted_iota(jnp.int32, (windows, samples), 0)
    flags = jnp.zeros((windows, samples), f32)
    for w in range(windows):
        flags = jnp.where(window == w, held_flag_ref[0, w].astype(f32), flags)
    early_ref[early * channels :] = jnp.concatenate([last[0], flags], axis=0).astype(bf16)


def travelling(flags, traces):
    channels, windows, samples = traces.shape
    step = 16
    early = early_windows(windows)
    return pl.pallas_call(
        functools.partial(block_kernel, step=step),
        in_specs=[pl.BlockSpec(memory_space=pltpu.HBM)] * 2,
        out_specs=(VMEM_SPEC,) * 2,
        out_shape=(
            jax.ShapeDtypeStruct((early * channels + EXTRA, samples), bf16),
            jax.ShapeDtypeStruct(((windows - early) * channels, samples), bf16),
        ),
        scratch_shapes=[
            VMEM(traces.shape, bf16),
            pltpu.SMEM(flags.shape, flags.dtype),
            pltpu.SemaphoreType.DMA((channels // step,)),
            pltpu.SemaphoreType.DMA,
        ],
        compiler_params=pltpu.CompilerParams(vmem_limit_bytes=52 * 2**20),
        cost_estimate=pl.CostEstimate(flops=10**10, bytes_accessed=2 * 2**20, transcendentals=0),
        name="travelling",
    )(flags, traces)


def extra_rows(piece_ref):
    extra = piece_ref[piece_ref.shape[0] - EXTRA :].astype(f32)
    return extra[: EXTRA // 2], extra[EXTRA // 2 :]


def less_before(tile, before):
    first = lax.broadcasted_iota(jnp.int32, tile.shape, 0) == 0
    tile = tile.astype(f32)
    return jnp.where(first, tile - before, tile).astype(bf16)


def left_kernel(early_ref, late_ref, before_ref, forward_ref, left_ref, block_ref, *, step, windows):
    early = early_windows(windows)
    channels = late_ref.shape[0] // (windows - early)
    samples = late_ref.shape[1]
    freqs = samples // 2
    k_own = 4 * windows
    lanes = k_own * F8
    per = step // 2
    same = (
        lax.broadcasted_iota(jnp.int32, (freqs, freqs), 0) // BAND
        == lax.broadcasted_iota(jnp.int32, (freqs, freqs), 1) // BAND
    )
    mean = jnp.where(same, 1.0 / BAND, 0.0).astype(bf16)
    before = before_ref[0].astype(f32)
    block_ref[: early * channels] = early_ref[: early * channels]
    block_ref[early * channels : windows * channels] = late_ref[...]
    block_ref[windows * channels :] = early_ref[early * channels :]
    _, flags = extra_rows(early_ref)
    usable = jnp.concatenate(
        [jnp.broadcast_to(flags[w : w + 1, :freqs], (step, freqs)) for w in range(windows)],
        axis=0,
    )
    row = lax.broadcasted_iota(jnp.int32, (2 * step * windows, lanes), 0)
    k = lax.broadcasted_iota(jnp.int32, (2 * step * windows, lanes), 1) // F8
    place = k // 4 % 2 * (step * windows) + (k // 8 * 2 + k % 2) * step + k // 2 % 2
    keep = (
        lax.broadcasted_iota(jnp.int32, (F8, lanes), 1) % F8
        == lax.broadcasted_iota(jnp.int32, (F8, lanes), 0)
    )[None]

    def chunk(s, _):
        base = s * step
        tiles = []
        for w in range(windows):
            at = (w if w < early else w - early) * channels
            tile = (early_ref if w < early else late_ref)[pl.ds(pl.multiple_of(at + base, step), step)]
            tiles.append(less_before(tile, jnp.where(s == 0, before[w : w + 1], 0.0)))
        spectra = dot_nt(jnp.concatenate(tiles, axis=0), forward_ref[...])
        power = spectra[:, :freqs] ** 2 + spectra[:, freqs:] ** 2
        high = power.astype(bf16)
        low = (power - high.astype(f32)).astype(bf16)
        level = dot(high, mean) + dot(low, mean)
        factor = lax.rsqrt(level + EPSILON) * usable
        parts = jnp.concatenate([spectra[:, :freqs] * factor, spectra[:, freqs:] * factor], axis=0)
        turned = parts.astype(bf16).T
        for pair in range(0, per, 2):
            both = []
            for q in range(2):
                spread = jnp.where(row == place + 2 * (pair + q), 1.0, 0.0).astype(bf16)
                wide = dot(turned, spread).reshape(freqs // F8, F8, lanes)
                both.append(jnp.where(keep, wide, 0.0))
            at = pl.multiple_of((s * per + pair) * F8, 2 * F8)
            left_ref[:, pl.ds(at, 2 * F8), :] = jnp.concatenate(both, axis=1).astype(bf16)
        return 0

    lax.fori_loop(0, channels // step, chunk, 0)


def left_side(early, late, before, forward, windows):
    samples = late.shape[1]
    channels = late.shape[0] // (windows - early_windows(windows))
    freqs = samples // 2
    return pl.pallas_call(
        functools.partial(left_kernel, step=16, windows=windows),
        in_specs=[VMEM_SPEC] * 4,
        out_specs=(VMEM_SPEC,) * 2,
        out_shape=(
            jax.ShapeDtypeStruct((freqs // F8, channels // 2 * F8, 4 * windows * F8), bf16),
            jax.ShapeDtypeStruct((windows * channels + EXTRA, samples), bf16),
        ),
        compiler_params=pltpu.CompilerParams(vmem_limit_bytes=28 * 2**20),
        cost_estimate=pl.CostEstimate(flops=10**11, bytes_accessed=12 * 2**20, transcendentals=0),
        name="left_side",
    )(early, late, before, forward)


def placed(index, even_rows, odd_rows):
    return odd_rows if even_rows is None else jnp.where(index % 2 == 0, even_rows, odd_rows)


def differences(rows, before, channels):
    tiles = []
    for w in range(rows.shape[0] // channels):
        tiles.append(less_before(rows[w * channels : w * channels + 16], before[w : w + 1]))
        tiles.append(rows[w * channels + 16 : (w + 1) * channels])
    return jnp.concatenate(tiles, axis=0)


def before_first(prior_ref, index, round_index):
    last, _ = extra_rows(prior_ref)
    return jnp.where(lax.rem(index + round_index, lax.axis_size("blk")) == 0, 0.0, last)


def window_pair_flags(flags, windows, half):
    first_half = lax.broadcasted_iota(jnp.int32, (1, 2 * half), 1) < half
    return [
        jnp.where(first_half, flags[w : w + 1, : 2 * half], flags[w + 1 : w + 2, : 2 * half])
        for w in range(0, windows, 2)
    ]


def whitened_pair(spectra_ref, band, at, usable):
    freqs = spectra_ref.shape[0] // 2
    start = band * BAND
    re = spectra_ref[start : start + BAND, at]
    im = spectra_ref[freqs + start : freqs + start + BAND, at]
    level = jnp.sum(re * re + im * im, axis=0, keepdims=True) * (1.0 / BAND)
    factor = lax.rsqrt(level + EPSILON) * usable
    return re * factor, im * factor


def right_kernel(odd_refs, even_refs, odd_flag_ref, even_flag_ref, prior_ref, forward_ref, right_ref, spectra_ref, *,
                 round_index, skip):
    samples = prior_ref.shape[1]
    freqs = samples // 2
    pairs = right_ref.shape[0]
    half = spectra_ref.shape[1] // (2 * pairs)
    index = lax.axis_index("blk")

    def rows_of(refs):
        rows = jnp.concatenate([ref[: ref.shape[0] // half * half] for ref in refs], axis=0)
        return rows[: 2 * pairs * half]

    here = placed(index, None if even_refs is None else rows_of(even_refs), rows_of(odd_refs))
    _, flags = extra_rows(odd_flag_ref)
    if even_flag_ref is not None:
        flags = placed(index, extra_rows(even_flag_ref)[1], flags)
    before = before_first(prior_ref, index, round_index)[skip:]
    spectra_ref[...] = dot_nt(forward_ref[...], differences(here, before, half))
    usable = window_pair_flags(flags[skip:], 2 * pairs, half)
    groups = BAND // F8
    lane = lax.broadcasted_iota(jnp.int32, (groups, F8, 2 * half), 2) < half
    for b in range(freqs // BAND):
        g = b * groups
        for w2 in range(pairs):
            tiles = []
            at = slice(w2 * 2 * half, (w2 + 1) * 2 * half)
            for part in whitened_pair(spectra_ref, b, at, usable[w2]):
                t = part.reshape(groups, F8, 2 * half)
                r = pltpu.roll(part, half, 1).reshape(groups, F8, 2 * half)
                p0 = jnp.concatenate([jnp.where(lane, t, 0.0), jnp.where(lane, r, 0.0)], axis=1)
                p1 = jnp.concatenate([jnp.where(lane, 0.0, r), jnp.where(lane, 0.0, t)], axis=1)
                tiles.append((p0.astype(bf16), p1.astype(bf16)))
            for p in range(2):
                for q in range(2):
                    rows = slice((2 * q + p) * 2 * F8, (2 * q + p + 1) * 2 * F8)
                    right_ref[w2, g : g + groups, rows, : 2 * half] = tiles[q][p]
                    right_ref[w2, g : g + groups, rows, 2 * half :] = tiles[1][p] if q == 0 else -tiles[0][p]


def right_side(round_index, mine, skip, odd, even, prior, forward_t):
    samples = prior.shape[1]
    freqs = samples // 2
    operands, places = [], []
    for array in odd + (even or []) + [prior, forward_t]:
        if not any(array is other for other in operands):
            operands.append(array)
        places.append(next(i for i, other in enumerate(operands) if other is array))
    channels = CH

    def kernel(*refs):
        named = [refs[i] for i in places]
        odd_refs = [named.pop(0) for _ in odd]
        even_refs = [named.pop(0) for _ in even or []]
        right_kernel(odd_refs[:-1], even_refs[:-1] or None, odd_refs[-1], even_refs[-1] if even else None, *named,
                     *refs[len(operands) :], round_index=round_index, skip=skip)

    return pl.pallas_call(
        kernel,
        in_specs=[VMEM_SPEC] * len(operands),
        out_specs=VMEM_SPEC,
        out_shape=jax.ShapeDtypeStruct((mine // 2, freqs // F8, 8 * F8, 4 * channels), bf16),
        scratch_shapes=[VMEM((samples, mine * channels), f32)],
        compiler_params=pltpu.CompilerParams(vmem_limit_bytes=20 * 2**20),
        cost_estimate=pl.CostEstimate(flops=2 * 10**9, bytes_accessed=5 * 2**20, transcendentals=0),
        name="right_side",
    )(*operands)


def pair_kernel(
    odd_early_ref, even_early_ref, own_ref, left_ref, right_refs, inverse_ref, *rest, round_index
):
    out_ref, cross_ref, lag_ref, sems = rest[-4:]
    channels = right_refs[0].shape[3] // 4
    samples = inverse_ref.shape[0]
    freqs = samples // 2
    half = channels
    groups = BAND // F8
    index = lax.axis_index("blk")
    _, far_flags = extra_rows(odd_early_ref)
    if even_early_ref is not None:
        far_flags = placed(index, extra_rows(even_early_ref)[1], far_flags)
    _, own_flags = extra_rows(own_ref)

    def cross(b):
        bands = freqs // BAND
        quarter = BAND // 4
        for pair in range(groups // 2):
            outs = []
            for e in range(2):
                g = b * groups + 2 * pair + e
                right = [ref[w2, g] for ref in right_refs for w2 in range(ref.shape[0])]
                product = dot(left_ref[g], jnp.concatenate(right, axis=0))
                outs.append(product.reshape(channels // 2, F8, 4 * half))
            both = jnp.concatenate(outs, axis=1).astype(bf16)
            kind = min(pair, 2)
            count = 1 if kind < 2 else 2
            row = 2 * kind * bands * quarter + (b * count + pair - kind) * quarter
            cross_ref[:, row : row + quarter, :] = both[:, :, : 2 * half]
            row += count * bands * quarter
            cross_ref[:, row : row + quarter, :] = both[:, :, 2 * half :]

    for b in range(freqs // BAND):
        cross(b)

    both_flags = own_flags[:, :LAGS] * far_flags[:, :LAGS]
    scale = 1.0 / jnp.maximum(jnp.sum(both_flags, axis=0, keepdims=True), 1.0)

    group = 4

    def copy(k):
        at = pl.ds(k * 2 * group, 2 * group)
        return pltpu.make_async_copy(lag_ref.at[at], out_ref.at[round_index - 1, 0, at], sems.at[k])

    copies = channels // 2 // group
    quarter = samples // 4
    near = LAGS // 2

    def lags(k, _):
        for u in range(LAG_UNROLL):
            n = k * LAG_UNROLL + u
            stacked = jnp.concatenate([cross_ref[n * group + e] for e in range(group)], axis=1)
            zero = dot_tn(stacked[:quarter], inverse_ref[:quarter, :near])
            two = dot_tn(stacked[quarter : 2 * quarter], inverse_ref[quarter : 2 * quarter, :near])
            odd = dot_tn(stacked[2 * quarter :], inverse_ref[2 * quarter :, :])
            result = jnp.concatenate([zero + two + odd[:, :near], zero - two + odd[:, near:]], axis=1) * scale
            lag_ref[pl.ds(n * 2 * group, 2 * group)] = result.astype(bf16).reshape(2 * group, channels, LAGS)
            copy(n).start()
        return 0

    lax.fori_loop(0, copies // LAG_UNROLL, lags, 0)

    def finish(k, _):
        copy(k).wait()
        return 0

    lax.fori_loop(0, copies, finish, 0)


LAG_UNROLL = 8


def correlate(round_index, odd, even, own, left, rights, inverse, out):
    channels = rights[0].shape[3] // 4
    samples = inverse.shape[0]
    operands = [odd] + ([even] if even is not None else []) + [own, left, *rights, inverse]
    in_specs = [VMEM_SPEC] * len(operands)
    aliases = {}
    if out is not None:
        operands.append(out)
        in_specs.append(pl.BlockSpec(memory_space=pl.ANY))
        aliases = {len(operands) - 1: 0}

    def kernel(odd_ref, *refs):
        refs = list(refs)
        even_ref = refs.pop(0) if even is not None else None
        own_ref, left_ref = refs.pop(0), refs.pop(0)
        right_refs = [refs.pop(0) for _ in rights]
        pair_kernel(odd_ref, even_ref, own_ref, left_ref, right_refs, *refs, round_index=round_index)

    return pl.pallas_call(
        kernel,
        in_specs=in_specs,
        out_specs=pl.BlockSpec(memory_space=pl.ANY),
        out_shape=jax.ShapeDtypeStruct((ROUNDS, 1, channels, channels, LAGS), bf16),
        scratch_shapes=[
            VMEM((channels // 2, samples, 2 * channels), bf16),
            VMEM((channels, channels, LAGS), bf16),
            pltpu.SemaphoreType.DMA((channels // 8,)),
        ],
        input_output_aliases=aliases,
        compiler_params=pltpu.CompilerParams(vmem_limit_bytes=20 * 2**20),
        cost_estimate=pl.CostEstimate(flops=7 * 10**9, bytes_accessed=20 * 2**20, transcendentals=0),
        name="correlate",
    )(*operands)


def shards(traces, valid):
    size = lax.axis_size("blk")
    channels, windows, samples = traces.shape
    forward_t = jnp.asarray(np.ascontiguousarray(forward_table(samples).T))
    inverse = jnp.asarray(inverse_table(samples))

    def permute(x, route):
        return lax.ppermute(x, "blk", route)

    ring = lambda d: [((i + d) % size, i) for i in range(size)]
    last, traces = lax.optimization_barrier((traces[channels - 1 :], traces))
    before = permute(last, [(i, i + 1) for i in range(size - 1)])
    early, late = travelling(valid, traces)
    to_odd = [((i + 2) % size, i) for i in range(1, size, 2)]
    swap = [(i ^ 1, i) for i in range(size)]
    first_early = permute(early, ring(1))
    before, late_sent = lax.optimization_barrier((before, late))
    first_late = permute(late_sent, ring(1))
    left, block = left_side(early, late, before, forward_t, windows)
    second = permute(block, to_odd)
    first_early, left = lax.optimization_barrier((first_early, left))
    relay_early = permute(first_early, swap)
    count = early_windows(windows)
    rights = [right_side(1, count, 0, [first_early, first_early], None, early, forward_t)]
    first_late, rights = lax.optimization_barrier((first_late, rights))
    relay_late = permute(first_late, swap)
    rights += [right_side(1, windows - count, count, [first_late, first_early], None, early, forward_t)]
    out = correlate(1, first_early, None, early, left, rights, inverse, None)

    relay = [relay_early, relay_late, relay_early]
    rights = [right_side(2, windows, 0, [second, second], relay, first_early, forward_t)]
    return correlate(2, second, relay_early, early, left, rights, inverse, out)


def solution(mesh):
    return jax.shard_map(
        shards,
        mesh=mesh,
        in_specs=(P(("days", "blk"), None, None), P(("days", "blk"), None)),
        out_specs=P(None, ("days", "blk"), None, None, None),
        check_vma=False,
    )
```

```python
import functools
import math

import jax
import jax.numpy as jnp
import ml_dtypes
import numpy as np
from jax import lax
from jax.experimental import pallas as pl
from jax.experimental.pallas import tpu as pltpu
from jax.sharding import PartitionSpec as P

CH = 64
LAGS = 512
BAND = 64
ROUNDS = 2
EPSILON = 1e-05
F8 = 8

f32 = jnp.float32
bf16 = jnp.bfloat16
VMEM = pltpu.VMEM


def bin_order(freqs):
    bins = np.arange(freqs).reshape(-1, BAND)
    kinds = [bins[:, bins[0] % 4 == 0], bins[:, bins[0] % 4 == 2], bins[:, bins[0] % 2 == 1]]
    return np.concatenate(kinds, axis=1).reshape(-1)


def forward_table(samples):
    bins = bin_order(samples // 2)
    phase = (np.arange(samples)[:, None] * bins[None, :]) % samples
    phase = phase * (2.0 * math.pi / samples)
    table = np.concatenate([np.cos(phase), -np.sin(phase)], axis=1) / math.sqrt(samples)
    return table.astype(np.float32).astype(ml_dtypes.bfloat16)


def inverse_table(samples):
    freqs = samples // 2
    bins = np.arange(freqs)
    shifts = np.arange(LAGS) - LAGS // 2
    phase = (bins[:, None] * shifts[None, :]) % samples
    phase = phase * (2.0 * math.pi / samples)
    weight = np.where(bins == 0, 1.0, 2.0)[:, None] / math.sqrt(freqs)
    parts = [weight * np.cos(phase), -weight * np.sin(phase)]
    kinds = [bins % 4 == 0, bins % 4 == 2, bins % 2 == 1]
    table = np.concatenate([part[kind] for kind in kinds for part in parts], axis=0)
    return table.astype(np.float32).astype(ml_dtypes.bfloat16)


def dot(a, b):
    return jnp.dot(a, b, preferred_element_type=f32)


def dot_nt(a, b):
    return lax.dot_general(a, b, (((1,), (1,)), ((), ())), preferred_element_type=f32)


def dot_tn(a, b):
    return lax.dot_general(a, b, (((0,), (0,)), ((), ())), preferred_element_type=f32)


SMEM_SPEC = pl.BlockSpec(memory_space=pltpu.SMEM)
VMEM_SPEC = pl.BlockSpec(memory_space=pltpu.VMEM)
EXTRA = 16


def early_windows(windows):
    return windows * 3 // 4


def block_kernel(flag_ref, trace_ref, early_ref, late_ref, held_ref, held_flag_ref, sems, flag_sem, *, step):
    channels, windows, samples = trace_ref.shape
    early = early_windows(windows)

    def copy(c):
        at = pl.ds(c * step, step)
        return pltpu.make_async_copy(trace_ref.at[at], held_ref.at[at], sems.at[c])

    flag_copy = pltpu.make_async_copy(flag_ref, held_flag_ref, flag_sem)
    for c in range(channels // step):
        copy(c).start()
    flag_copy.start()
    last = None
    for c in range(channels // step):
        copy(c).wait()
        here = held_ref[c * step : (c + 1) * step].astype(f32)
        before = jnp.zeros_like(here[:1]) if last is None else last
        diffed = here - jnp.concatenate([before, here[:-1]], axis=0)
        last = here[step - 1 :]
        turned = jnp.swapaxes(diffed, 0, 1).astype(bf16)
        for w in range(windows):
            row = (w if w < early else w - early) * channels + c * step
            (early_ref if w < early else late_ref)[row : row + step] = turned[w]
    flag_copy.wait()
    window = lax.broadcasted_iota(jnp.int32, (windows, samples), 0)
    flags = jnp.zeros((windows, samples), f32)
    for w in range(windows):
        flags = jnp.where(window == w, held_flag_ref[0, w].astype(f32), flags)
    early_ref[early * channels :] = jnp.concatenate([last[0], flags], axis=0).astype(bf16)


def travelling(flags, traces):
    channels, windows, samples = traces.shape
    step = 16
    early = early_windows(windows)
    return pl.pallas_call(
        functools.partial(block_kernel, step=step),
        in_specs=[pl.BlockSpec(memory_space=pltpu.HBM)] * 2,
        out_specs=(VMEM_SPEC,) * 2,
        out_shape=(
            jax.ShapeDtypeStruct((early * channels + EXTRA, samples), bf16),
            jax.ShapeDtypeStruct(((windows - early) * channels, samples), bf16),
        ),
        scratch_shapes=[
            VMEM(traces.shape, bf16),
            pltpu.SMEM(flags.shape, flags.dtype),
            pltpu.SemaphoreType.DMA((channels // step,)),
            pltpu.SemaphoreType.DMA,
        ],
        compiler_params=pltpu.CompilerParams(vmem_limit_bytes=52 * 2**20),
        cost_estimate=pl.CostEstimate(flops=10**10, bytes_accessed=2 * 2**20, transcendentals=0),
        name="travelling",
    )(flags, traces)


def extra_rows(piece_ref):
    extra = piece_ref[piece_ref.shape[0] - EXTRA :].astype(f32)
    return extra[: EXTRA // 2], extra[EXTRA // 2 :]


def less_before(tile, before):
    first = lax.broadcasted_iota(jnp.int32, tile.shape, 0) == 0
    tile = tile.astype(f32)
    return jnp.where(first, tile - before, tile).astype(bf16)


def left_kernel(early_ref, late_ref, before_ref, forward_ref, left_ref, block_ref, *, step, windows):
    early = early_windows(windows)
    channels = late_ref.shape[0] // (windows - early)
    samples = late_ref.shape[1]
    freqs = samples // 2
    k_own = 4 * windows
    lanes = k_own * F8
    per = step // 2
    same = (
        lax.broadcasted_iota(jnp.int32, (freqs, freqs), 0) // BAND
        == lax.broadcasted_iota(jnp.int32, (freqs, freqs), 1) // BAND
    )
    mean = jnp.where(same, 1.0 / BAND, 0.0).astype(bf16)
    before = before_ref[0].astype(f32)
    block_ref[: early * channels] = early_ref[: early * channels]
    block_ref[early * channels : windows * channels] = late_ref[...]
    block_ref[windows * channels :] = early_ref[early * channels :]
    _, flags = extra_rows(early_ref)
    usable = jnp.concatenate(
        [jnp.broadcast_to(flags[w : w + 1, :freqs], (step, freqs)) for w in range(windows)],
        axis=0,
    )
    row = lax.broadcasted_iota(jnp.int32, (2 * step * windows, lanes), 0)
    k = lax.broadcasted_iota(jnp.int32, (2 * step * windows, lanes), 1) // F8
    place = k // 4 % 2 * (step * windows) + (k // 8 * 2 + k % 2) * step + k // 2 % 2
    keep = (
        lax.broadcasted_iota(jnp.int32, (F8, lanes), 1) % F8
        == lax.broadcasted_iota(jnp.int32, (F8, lanes), 0)
    )[None]

    def chunk(s, _):
        base = s * step
        tiles = []
        for w in range(windows):
            at = (w if w < early else w - early) * channels
            tile = (early_ref if w < early else late_ref)[pl.ds(pl.multiple_of(at + base, step), step)]
            tiles.append(less_before(tile, jnp.where(s == 0, before[w : w + 1], 0.0)))
        spectra = dot_nt(jnp.concatenate(tiles, axis=0), forward_ref[...])
        power = spectra[:, :freqs] ** 2 + spectra[:, freqs:] ** 2
        high = power.astype(bf16)
        low = (power - high.astype(f32)).astype(bf16)
        level = dot(high, mean) + dot(low, mean)
        factor = lax.rsqrt(level + EPSILON) * usable
        parts = jnp.concatenate([spectra[:, :freqs] * factor, spectra[:, freqs:] * factor], axis=0)
        turned = parts.astype(bf16).T
        for pair in range(0, per, 2):
            both = []
            for q in range(2):
                spread = jnp.where(row == place + 2 * (pair + q), 1.0, 0.0).astype(bf16)
                wide = dot(turned, spread).reshape(freqs // F8, F8, lanes)
                both.append(jnp.where(keep, wide, 0.0))
            at = pl.multiple_of((s * per + pair) * F8, 2 * F8)
            left_ref[:, pl.ds(at, 2 * F8), :] = jnp.concatenate(both, axis=1).astype(bf16)
        return 0

    def two(s, _):
        chunk(2 * s, 0)
        chunk(2 * s + 1, 0)
        return 0

    lax.fori_loop(0, channels // step // 2, two, 0)


def left_side(early, late, before, forward, windows):
    samples = late.shape[1]
    channels = late.shape[0] // (windows - early_windows(windows))
    freqs = samples // 2
    return pl.pallas_call(
        functools.partial(left_kernel, step=16, windows=windows),
        in_specs=[VMEM_SPEC] * 4,
        out_specs=(VMEM_SPEC,) * 2,
        out_shape=(
            jax.ShapeDtypeStruct((freqs // F8, channels // 2 * F8, 4 * windows * F8), bf16),
            jax.ShapeDtypeStruct((windows * channels + EXTRA, samples), bf16),
        ),
        compiler_params=pltpu.CompilerParams(vmem_limit_bytes=28 * 2**20),
        cost_estimate=pl.CostEstimate(flops=10**11, bytes_accessed=12 * 2**20, transcendentals=0),
        name="left_side",
    )(early, late, before, forward)


def placed(index, even_rows, odd_rows):
    return odd_rows if even_rows is None else jnp.where(index % 2 == 0, even_rows, odd_rows)


def differences(rows, before, channels):
    tiles = []
    for w in range(rows.shape[0] // channels):
        tiles.append(less_before(rows[w * channels : w * channels + 16], before[w : w + 1]))
        tiles.append(rows[w * channels + 16 : (w + 1) * channels])
    return jnp.concatenate(tiles, axis=0)


def before_first(prior_ref, index, round_index):
    last, _ = extra_rows(prior_ref)
    return jnp.where(lax.rem(index + round_index, lax.axis_size("blk")) == 0, 0.0, last)


def window_pair_flags(flags, windows, half):
    first_half = lax.broadcasted_iota(jnp.int32, (1, 2 * half), 1) < half
    return [
        jnp.where(first_half, flags[w : w + 1, : 2 * half], flags[w + 1 : w + 2, : 2 * half])
        for w in range(0, windows, 2)
    ]


def whitened_pair(spectra_ref, band, at, usable):
    freqs = spectra_ref.shape[0] // 2
    start = band * BAND
    re = spectra_ref[start : start + BAND, at]
    im = spectra_ref[freqs + start : freqs + start + BAND, at]
    level = jnp.sum(re * re + im * im, axis=0, keepdims=True) * (1.0 / BAND)
    factor = lax.rsqrt(level + EPSILON) * usable
    return re * factor, im * factor


def right_kernel(odd_refs, even_refs, odd_flag_ref, even_flag_ref, prior_ref, forward_ref, right_ref, spectra_ref, *,
                 round_index, skip):
    samples = prior_ref.shape[1]
    freqs = samples // 2
    pairs = right_ref.shape[0]
    half = spectra_ref.shape[1] // (2 * pairs)
    index = lax.axis_index("blk")

    def rows_of(refs):
        rows = jnp.concatenate([ref[: ref.shape[0] // half * half] for ref in refs], axis=0)
        return rows[: 2 * pairs * half]

    here = placed(index, None if even_refs is None else rows_of(even_refs), rows_of(odd_refs))
    _, flags = extra_rows(odd_flag_ref)
    if even_flag_ref is not None:
        flags = placed(index, extra_rows(even_flag_ref)[1], flags)
    before = before_first(prior_ref, index, round_index)[skip:]
    spectra_ref[...] = dot_nt(forward_ref[...], differences(here, before, half))
    usable = window_pair_flags(flags[skip:], 2 * pairs, half)
    groups = BAND // F8
    lane = lax.broadcasted_iota(jnp.int32, (groups, F8, 2 * half), 2) < half
    for b in range(freqs // BAND):
        g = b * groups
        for w2 in range(pairs):
            tiles = []
            at = slice(w2 * 2 * half, (w2 + 1) * 2 * half)
            for part in whitened_pair(spectra_ref, b, at, usable[w2]):
                t = part.reshape(groups, F8, 2 * half)
                r = pltpu.roll(part, half, 1).reshape(groups, F8, 2 * half)
                p0 = jnp.concatenate([jnp.where(lane, t, 0.0), jnp.where(lane, r, 0.0)], axis=1)
                p1 = jnp.concatenate([jnp.where(lane, 0.0, r), jnp.where(lane, 0.0, t)], axis=1)
                tiles.append((p0.astype(bf16), p1.astype(bf16)))
            for p in range(2):
                for q in range(2):
                    rows = slice((2 * q + p) * 2 * F8, (2 * q + p + 1) * 2 * F8)
                    right_ref[w2, g : g + groups, rows, : 2 * half] = tiles[q][p]
                    right_ref[w2, g : g + groups, rows, 2 * half :] = tiles[1][p] if q == 0 else -tiles[0][p]


def right_side(round_index, mine, skip, odd, even, prior, forward_t):
    samples = prior.shape[1]
    freqs = samples // 2
    operands, places = [], []
    for array in odd + (even or []) + [prior, forward_t]:
        if not any(array is other for other in operands):
            operands.append(array)
        places.append(next(i for i, other in enumerate(operands) if other is array))
    channels = CH

    def kernel(*refs):
        named = [refs[i] for i in places]
        odd_refs = [named.pop(0) for _ in odd]
        even_refs = [named.pop(0) for _ in even or []]
        right_kernel(odd_refs[:-1], even_refs[:-1] or None, odd_refs[-1], even_refs[-1] if even else None, *named,
                     *refs[len(operands) :], round_index=round_index, skip=skip)

    return pl.pallas_call(
        kernel,
        in_specs=[VMEM_SPEC] * len(operands),
        out_specs=VMEM_SPEC,
        out_shape=jax.ShapeDtypeStruct((mine // 2, freqs // F8, 8 * F8, 4 * channels), bf16),
        scratch_shapes=[VMEM((samples, mine * channels), f32)],
        compiler_params=pltpu.CompilerParams(vmem_limit_bytes=20 * 2**20),
        cost_estimate=pl.CostEstimate(flops=2 * 10**9, bytes_accessed=5 * 2**20, transcendentals=0),
        name="right_side",
    )(*operands)


def pair_kernel(
    odd_early_ref, even_early_ref, own_ref, left_ref, right_refs, inverse_ref, *rest, round_index
):
    out_ref, cross_ref, lag_ref, sems = rest[-4:]
    channels = right_refs[0].shape[3] // 4
    samples = inverse_ref.shape[0]
    freqs = samples // 2
    half = channels
    groups = BAND // F8
    index = lax.axis_index("blk")
    _, far_flags = extra_rows(odd_early_ref)
    if even_early_ref is not None:
        far_flags = placed(index, extra_rows(even_early_ref)[1], far_flags)
    _, own_flags = extra_rows(own_ref)

    def cross(b):
        bands = freqs // BAND
        quarter = BAND // 4
        for pair in range(groups // 2):
            outs = []
            for e in range(2):
                g = b * groups + 2 * pair + e
                right = [ref[w2, g] for ref in right_refs for w2 in range(ref.shape[0])]
                product = dot(left_ref[g], jnp.concatenate(right, axis=0))
                outs.append(product.reshape(channels // 2, F8, 4 * half))
            both = jnp.concatenate(outs, axis=1).astype(bf16)
            kind = min(pair, 2)
            count = 1 if kind < 2 else 2
            row = 2 * kind * bands * quarter + (b * count + pair - kind) * quarter
            cross_ref[:, row : row + quarter, :] = both[:, :, : 2 * half]
            row += count * bands * quarter
            cross_ref[:, row : row + quarter, :] = both[:, :, 2 * half :]

    for b in range(freqs // BAND):
        cross(b)

    both_flags = own_flags[:, :LAGS] * far_flags[:, :LAGS]
    scale = 1.0 / jnp.maximum(jnp.sum(both_flags, axis=0, keepdims=True), 1.0)

    group = 4

    def copy(k):
        at = pl.ds(k * 2 * group, 2 * group)
        return pltpu.make_async_copy(lag_ref.at[at], out_ref.at[round_index - 1, 0, at], sems.at[k])

    copies = channels // 2 // group
    quarter = samples // 4
    near = LAGS // 2

    def lags(k, _):
        for u in range(LAG_UNROLL):
            n = k * LAG_UNROLL + u
            stacked = jnp.concatenate([cross_ref[n * group + e] for e in range(group)], axis=1)
            zero = dot_tn(stacked[:quarter], inverse_ref[:quarter, :near])
            two = dot_tn(stacked[quarter : 2 * quarter], inverse_ref[quarter : 2 * quarter, :near])
            odd = dot_tn(stacked[2 * quarter :], inverse_ref[2 * quarter :, :])
            result = jnp.concatenate([zero + two + odd[:, :near], zero - two + odd[:, near:]], axis=1) * scale
            lag_ref[pl.ds(n * 2 * group, 2 * group)] = result.astype(bf16).reshape(2 * group, channels, LAGS)
            copy(n).start()
        return 0

    lax.fori_loop(0, copies // LAG_UNROLL, lags, 0)

    def finish(k, _):
        copy(k).wait()
        return 0

    lax.fori_loop(0, copies, finish, 0)


LAG_UNROLL = 8


def correlate(round_index, odd, even, own, left, rights, inverse, out):
    channels = rights[0].shape[3] // 4
    samples = inverse.shape[0]
    operands = [odd] + ([even] if even is not None else []) + [own, left, *rights, inverse]
    in_specs = [VMEM_SPEC] * len(operands)
    aliases = {}
    if out is not None:
        operands.append(out)
        in_specs.append(pl.BlockSpec(memory_space=pl.ANY))
        aliases = {len(operands) - 1: 0}

    def kernel(odd_ref, *refs):
        refs = list(refs)
        even_ref = refs.pop(0) if even is not None else None
        own_ref, left_ref = refs.pop(0), refs.pop(0)
        right_refs = [refs.pop(0) for _ in rights]
        pair_kernel(odd_ref, even_ref, own_ref, left_ref, right_refs, *refs, round_index=round_index)

    return pl.pallas_call(
        kernel,
        in_specs=in_specs,
        out_specs=pl.BlockSpec(memory_space=pl.ANY),
        out_shape=jax.ShapeDtypeStruct((ROUNDS, 1, channels, channels, LAGS), bf16),
        scratch_shapes=[
            VMEM((channels // 2, samples, 2 * channels), bf16),
            VMEM((channels, channels, LAGS), bf16),
            pltpu.SemaphoreType.DMA((channels // 8,)),
        ],
        input_output_aliases=aliases,
        compiler_params=pltpu.CompilerParams(vmem_limit_bytes=20 * 2**20),
        cost_estimate=pl.CostEstimate(flops=7 * 10**9, bytes_accessed=20 * 2**20, transcendentals=0),
        name="correlate",
    )(*operands)


def shards(traces, valid):
    size = lax.axis_size("blk")
    channels, windows, samples = traces.shape
    forward_t = jnp.asarray(np.ascontiguousarray(forward_table(samples).T))
    inverse = jnp.asarray(inverse_table(samples))

    def permute(x, route):
        return lax.ppermute(x, "blk", route)

    ring = lambda d: [((i + d) % size, i) for i in range(size)]
    last, traces = lax.optimization_barrier((traces[channels - 1 :], traces))
    before = permute(last, [(i, i + 1) for i in range(size - 1)])
    early, late = travelling(valid, traces)
    to_odd = [((i + 2) % size, i) for i in range(1, size, 2)]
    swap = [(i ^ 1, i) for i in range(size)]
    first_early = permute(early, ring(1))
    before, late_sent = lax.optimization_barrier((before, late))
    first_late = permute(late_sent, ring(1))
    left, block = left_side(early, late, before, forward_t, windows)
    second = permute(block, to_odd)
    first_early, left = lax.optimization_barrier((first_early, left))
    relay_early = permute(first_early, swap)
    count = early_windows(windows)
    rights = [right_side(1, count, 0, [first_early, first_early], None, early, forward_t)]
    first_late, rights = lax.optimization_barrier((first_late, rights))
    relay_late = permute(first_late, swap)
    rights += [right_side(1, windows - count, count, [first_late, first_early], None, early, forward_t)]
    out = correlate(1, first_early, None, early, left, rights, inverse, None)

    relay = [relay_early, relay_late, relay_early]
    rights = [right_side(2, windows, 0, [second, second], relay, first_early, forward_t)]
    return correlate(2, second, relay_early, early, left, rights, inverse, out)


def solution(mesh):
    return jax.shard_map(
        shards,
        mesh=mesh,
        in_specs=(P(("days", "blk"), None, None), P(("days", "blk"), None)),
        out_specs=P(None, ("days", "blk"), None, None, None),
        check_vma=False,
    )
```
